32 devices in a mesh: gy: 8 (over z, x), gz: 4 (over y, core).
Axes of the slice: x: 2, y: 2, z: 4, core: 2. Of those that a mesh axis runs over, the one named last changes fastest.
Arguments:
- density_seed: int32 [8, 512, 512], P(None, 'gy', 'gz'), may hold values from 0 to 15
- heat_load: float32 [8, 8, 512, 512], P(None, None, 'gy', 'gz'), may hold values from 0.3 to 3
- source_mask: int32 [8, 512, 512], P(None, 'gy', 'gz'), may hold values from 0 to 1, as said below
- fixed_mask: int32 [8, 512, 512], P(None, 'gy', 'gz'), may hold values 0 or 1
Outputs:
- temperature: float32 [8, 8, 512, 512], P(None, None, 'gy', 'gz')
- sensitivity: float32 [8, 512, 512], P(None, 'gy', 'gz')
The draws below stay inside these ranges and needn't reach their ends.
Inputs may be any that keep to these rules, and one draw needn't show every extreme that they name: `source_mask`: 1 marks a node with a heat source, 0 a node without.
All inputs are finite; a program needn't handle non-finite values. No bound on the sum of `fixed_mask` on one device may be relied on, other than what follows from the above.
Results may differ from the reference program's by a relative error of at most 0.0055.
Values sent between devices are 32-bit elements; how exact they have to be, the bound alone decides.
A program may use at most 128 MiB of HBM per device.

```python
import math
import jax
import jax.numpy as jnp
from jax import lax

LOADS = 8
ITERS = 4
NX = 8
NY = 512
NZ = 512


def draw_source_mask(key, part):
    key = jax.random.fold_in(key, 7)
    tile_key, force_key, cell_key = jax.random.split(key, 3)
    levels = jnp.maximum(jax.random.randint(tile_key, (4, 4), -4, 16), 0)
    forced = jax.random.randint(force_key, (), 0, 16)
    places = jnp.arange(16, dtype=jnp.int32).reshape(4, 4)
    levels = jnp.where(places == forced, 15, levels)
    rates = jnp.repeat(jnp.repeat(levels, NY // 4, axis=0), NZ // 4, axis=1)
    cells = jax.random.randint(cell_key, (NX, NY, NZ), 0, 16)
    return (cells < rates[None]).astype(jnp.int32)


def place_ends(entries, rng, low, high):
    shape = entries.shape
    spot = [jax.random.randint(jax.random.fold_in(rng, axis), (), 0, shape[axis]) for axis in range(len(shape))]
    entries = entries.at[tuple(spot)].set(low)
    longest = shape.index(max(shape))
    spot[longest] = (spot[longest] + 1) % shape[longest]
    return entries.at[tuple(spot)].set(high)


def shard_levels(rng, extent, pieces, least, largest):
    factor_of = 1.0
    for position, blocks in pieces:
        draws = jax.random.uniform(jax.random.fold_in(jax.random.fold_in(rng, 6), position), (blocks,), jnp.float32, least / len(pieces), largest / len(pieces))
        factor_of = factor_of * jnp.repeat(jnp.exp(draws), extent[position] // blocks).reshape((-1,) + (1,) * (len(extent) - 1 - position))
    return factor_of


def setup_inputs(seed: int = 0) -> dict:
    keys = jax.random.split(jax.random.key(seed), 5)
    density_seed = place_ends(jax.random.randint(keys[0], (NX, NY, NZ), 0, 16), jax.random.fold_in(keys[0], 1), 0, 15).astype(jnp.int32)
    heat_load = jnp.clip(jnp.exp(math.log(3.0) - 2.3025851 * jax.random.uniform(keys[1], (LOADS, NX, NY, NZ), jnp.float32) ** shard_levels(keys[1], (LOADS, NX, NY, NZ), ((2, 8), (3, 4)), -0.2, 0.2)), 0.3, 3.0)
    source_mask = draw_source_mask(jax.random.fold_in(keys[4], 71), 0)
    fixed_mask = place_ends((jax.random.randint(keys[3], (NX, NY, NZ), 0, 8) < 1).astype(jnp.int32), jax.random.fold_in(keys[3], 1), 0, 1)
    return dict(density_seed=density_seed, heat_load=heat_load, source_mask=source_mask, fixed_mask=fixed_mask)


cond_floor = 0.01
filter_weights = (1.0, 2.0, 3.0, 4.0, 3.0, 2.0, 1.0)
unit_corners = tuple((first, second, third) for first in (0, 1) for second in (0, 1) for third in (0, 1))


def coupling(count):
    if count == 0:
        return 1.0 / 3.0
    if count == 1:
        return 0.0
    return -1.0 / 12.0


def differ(corner, other):
    return sum(int(corner[place] != other[place]) for place in range(3))


def cut_nodes(padded, offset, shape3):
    return padded[..., 1 + offset[0]:1 + offset[0] + shape3[0], 1 + offset[1]:1 + offset[1] + shape3[1], 1 + offset[2]:1 + offset[2] + shape3[2]]


def conduct(field_pad, cond_pad, shape3):
    result = jnp.zeros((field_pad.shape[0],) + shape3, jnp.float32)
    for corner in unit_corners:
        element = tuple(-value for value in corner)
        cond = cut_nodes(cond_pad, element, shape3)
        inner = jnp.zeros_like(result)
        for other in unit_corners:
            weight = coupling(differ(corner, other))
            if weight == 0.0:
                continue
            offset = tuple(element[place] + other[place] for place in range(3))
            inner = inner + weight * cut_nodes(field_pad, offset, shape3)
        result = result + cond[None] * inner
    return result


def cond_total(cond_pad, shape3):
    total = jnp.zeros(shape3, jnp.float32)
    for corner in unit_corners:
        element = tuple(-value for value in corner)
        total = total + cut_nodes(cond_pad, element, shape3)
    return total


def energy(field_pad, shape3):
    result = jnp.zeros((field_pad.shape[0],) + shape3, jnp.float32)
    for corner in unit_corners:
        left = cut_nodes(field_pad, corner, shape3)
        for other in unit_corners:
            weight = coupling(differ(corner, other))
            if weight == 0.0:
                continue
            result = result + weight * left * cut_nodes(field_pad, other, shape3)
    return jnp.mean(result, axis=0)


def filter_mass(index, total):
    mass = jnp.zeros(index.shape, jnp.float32)
    for step in range(-3, 4):
        inside = ((index + step >= 0) & (index + step < total)).astype(jnp.float32)
        mass = mass + (4.0 - abs(step)) * inside
    return mass


def smooth(array, axis, count):
    result = filter_weights[0] * lax.slice_in_dim(array, 0, count, axis=axis)
    for step in range(1, 7):
        result = result + filter_weights[step] * lax.slice_in_dim(array, step, step + count, axis=axis)
    return result


def reference(density_seed, heat_load, source_mask, fixed_mask):
    shape3 = density_seed.shape
    density = (density_seed.astype(jnp.float32) + 1.0) / 16.0
    conductivity = cond_floor + (1.0 - cond_floor) * density ** 3
    free = 1.0 - fixed_mask.astype(jnp.float32)
    cond_pad = jnp.pad(conductivity, 1)
    diagonal = free * cond_total(cond_pad, shape3) / 3.0 + (1.0 - free)
    inverse = 1.0 / diagonal
    rhs = heat_load * (source_mask.astype(jnp.float32) * free)[None]
    widths = ((0, 0), (1, 1), (1, 1), (1, 1))

    def operate(vector):
        padded = jnp.pad(vector * free[None], widths)
        return free[None] * conduct(padded, cond_pad, shape3) + (1.0 - free)[None] * vector

    def inner_sum(left, right):
        return jnp.sum(left * right, axis=(1, 2, 3))[:, None, None, None]

    solution = jnp.zeros_like(rhs)
    residual = rhs
    precond = residual * inverse[None]
    direction = precond
    search = inner_sum(residual, precond)
    for step in range(ITERS):
        image = operate(direction)
        alpha = search / inner_sum(direction, image)
        solution = solution + alpha * direction
        residual = residual - alpha * image
        precond = residual * inverse[None]
        search_next = inner_sum(residual, precond)
        direction = precond + (search_next / search) * direction
        search = search_next
    mean_energy = energy(jnp.pad(solution, widths), shape3)
    raw = -3.0 * (1.0 - cond_floor) * density ** 2 * mean_energy
    mass_x = filter_mass(jnp.arange(NX, dtype=jnp.int32), NX)
    mass_y = filter_mass(jnp.arange(NY, dtype=jnp.int32), NY)
    mass_z = filter_mass(jnp.arange(NZ, dtype=jnp.int32), NZ)
    mass = mass_x[:, None, None] * mass_y[None, :, None] * mass_z[None, None, :]
    scaled = jnp.pad(raw / mass, 3)
    result = smooth(scaled, 0, NX)
    result = smooth(result, 1, NY)
    result = smooth(result, 2, NZ)
    return solution, result
```

```python
import functools

import jax
import jax.numpy as jnp
from jax import lax
from jax.experimental import pallas as pl
from jax.experimental.pallas import tpu as pltpu
from jax.sharding import PartitionSpec as P

STEPS = 4
L, X = 8, 8
R, Z = 64, 128
LO, HI, RP = 8, 72, 80
MESH = pl.DeviceIdType.MESH
FLOOR = 0.01
HALF = 0.75

NEAR = ((1, 0), (-1, 0), (0, 1), (0, -1), (1, 1), (1, -1), (-1, 1), (-1, -1))


def roll(v, shift):
    if isinstance(shift, int):
        shift = shift % 128
        if shift == 0:
            return v
    return pltpu.roll(v, shift, v.ndim - 1)


def kernel(ny, nz, seed, heat, source, fixed, temp, sens,
           U, BL, BO, BH, ELO, EHI, ETOP, EBOT, W, WC,
           C1, C2, C3, INV, DIAG, PS, ACC, RED, COEF,
           BC, BCL, CTOP, CLO, S, SLO, SHI, PZ, PZL, PZH, PM,
           AZ, AY, send, recv, rsend, rrecv):
    my_y, my_z = lax.axis_index("gy"), lax.axis_index("gz")
    f32 = jnp.float32
    lane = lax.broadcasted_iota(jnp.int32, (8, Z), 1)
    sub = lax.broadcasted_iota(jnp.int32, (8, Z), 0)
    lane16 = lax.rem(lane, 16)
    group = lax.div(lane, 16)
    zero = jnp.zeros((8, Z), f32)
    chunks = tuple(range(LO, HI, 8))

    def inside(dy, dz):
        ok = None
        for d, me, n in ((dy, my_y, ny), (dz, my_z, nz)):
            if d:
                this = (me + d >= 0) & (me + d < n)
                ok = this if ok is None else ok & this
        return ok

    for ref in (BL, BO, BH):
        ref[...] = jnp.zeros(ref.shape, f32)
    for ref in (ELO, EHI, BCL, CLO, SLO, SHI, PZL, PZH, C1, C2, C3, W):
        ref[...] = jnp.zeros(ref.shape, f32)

    barrier = pltpu.get_barrier_semaphore()
    for d in range(1, nz):
        pl.semaphore_signal(barrier, inc=1, device_id=(my_y, lax.rem(my_z + d, nz)), device_id_type=MESH)
    for d in range(1, ny):
        pl.semaphore_signal(barrier, inc=1, device_id=(lax.rem(my_y + d, ny), my_z), device_id_type=MESH)
    for dy, dz in NEAR[4:]:
        @pl.when(inside(dy, dz))
        def _(dy=dy, dz=dz):
            pl.semaphore_signal(barrier, inc=1, device_id=(my_y + dy, my_z + dz), device_id_type=MESH)

    for x in range(X):
        for r in range(0, R, 8):
            density = (seed[x, r:r + 8, :].astype(f32) + 1.0) / 16.0
            cond = (FLOOR + (1.0 - FLOOR) * (density * density * density)) * (1.0 / 48.0)
            C1[x, LO + r:LO + r + 8, :] = cond * 3.0
            C2[x, LO + r:LO + r + 8, :] = cond * 2.0
            C3[x, LO + r:LO + r + 8, :] = cond
            if r == R - 8:
                CTOP[x:x + 1, :] = cond[7:8, :]
    for r in range(LO, HI, 8):
        b = zero
        for x in range(X):
            b = jnp.where(lane16 >= 2 * x, roll(C3[x, r:r + 8, :], 2 * x + 1), b)
        b = jnp.where(group == 0, b, 0.0)
        for s in (16, 32, 64):
            b = b + roll(b, s)
        BC[r - LO:r - LO + 8, :] = b

    def sides(me, n):
        return jnp.where(me > 0, 1, 0) + jnp.where(me + 1 < n, 1, 0)

    pl.semaphore_wait(barrier, nz - 1 + ny - 1 + sides(my_y, ny) * sides(my_z, nz))

    def exchange(e, messages, start):
        for i, (dy, dz, src, dst) in enumerate(messages):
            def copy(dy=dy, dz=dz, src=src, dst=dst, i=i):
                return pltpu.make_async_remote_copy(
                    src_ref=src, dst_ref=dst, send_sem=send.at[e, i], recv_sem=recv.at[e, i],
                    device_id=(my_y + dy, my_z + dz), device_id_type=MESH)
            if start:
                @pl.when(inside(dy, dz))
                def _(copy=copy):
                    copy().start()
            else:
                @pl.when(inside(dy, dz))
                def _(copy=copy):
                    copy().wait_send()
                @pl.when(inside(-dy, -dz))
                def _(copy=copy):
                    copy().wait_recv()

    low, high = pl.ds(0, 8), pl.ds(HI, 8)
    first, last, mid = pl.ds(LO, 8), pl.ds(HI - 8, 8), pl.ds(LO, R)

    def halo(j):
        own = BO.at[j]
        return (
            (1, 0, ETOP.at[j], ELO.at[j]), (-1, 0, EBOT.at[j], EHI.at[j]),
            (0, 1, own.at[mid], BL.at[j].at[mid]), (0, -1, own.at[mid], BH.at[j].at[mid]),
            (1, 0, own.at[last], BO.at[j].at[low]), (-1, 0, own.at[first], BO.at[j].at[high]),
            (1, 1, own.at[last], BL.at[j].at[low]), (1, -1, own.at[last], BH.at[j].at[low]),
            (-1, 1, own.at[first], BL.at[j].at[high]), (-1, -1, own.at[first], BH.at[j].at[high]),
        )

    cond_messages = (
        (1, 0, CTOP, CLO),
        (0, 1, BC, BCL.at[mid]),
        (1, 1, BC.at[pl.ds(R - 8, 8)], BCL.at[low]),
    )
    exchange(STEPS, cond_messages, True)
    exchange(STEPS, cond_messages, False)
    for x in range(X):
        for ref, k in ((C1, 3.0), (C2, 2.0), (C3, 1.0)):
            ref[x, LO - 1:LO, :] = CLO[x:x + 1, :] * k

    for r in chunks:
        low_z = BCL[r:r + 8, :] + BCL[r - 1:r + 7, :]
        low_z = low_z + jnp.where(lane16 >= 2, roll(low_z, 2), 0.0)
        before = None
        for x in range(X):
            t = C3[x, r:r + 8, :] + C3[x, r - 1:r + 7, :]
            both = t if before is None else t + before
            before = t
            below = jnp.where(lane == 0, roll(low_z, -2 * x), roll(both, 1))
            total = (both + below) * 48.0 / 3.0
            free = 1.0 - fixed[x, r - LO:r - LO + 8, :].astype(f32)
            DIAG[x, r - LO:r - LO + 8, :] = total
            INV[x, r - LO:r - LO + 8, :] = free / total

    def pack_tail(j, l, r, b):
        BO[j, r:r + 8, :] = jnp.where(group == l, b, BO[j, r:r + 8, :])

    def edges(j, l, x, r, v):
        if r == LO:
            EBOT[j, l, x:x + 1, :] = v[0:1, :]
        if r == HI - 8:
            ETOP[j, l, x:x + 1, :] = v[7:8, :]

    @pl.loop(0, L)
    def _(l):
        acc = zero
        for r in chunks:
            b = zero
            q = r - LO
            for x in range(X):
                inv = INV[x, q:q + 8, :]
                rhs = heat[l, x, q:q + 8, :] * source[x, q:q + 8, :].astype(f32)
                v = rhs * inv
                U[0, l, x, r:r + 8, :] = v
                acc = acc + v * v * DIAG[x, q:q + 8, :]
                b = jnp.where(lane16 >= 2 * x, roll(v, 16 * l + 2 * x + 1), b)
                edges(0, l, x, r, v)
            pack_tail(0, l, r, b)
        ACC[0, l] = acc
    exchange(0, halo(0), True)

    def fill(j):
        @pl.loop(0, L)
        def _(l):
            for x in range(X):
                U[j, l, x, LO - 1:LO, :] = ELO[j, l, x:x + 1, :]
                U[j, l, x, HI:HI + 1, :] = EHI[j, l, x:x + 1, :]

        def up_x(v):
            return jnp.where(lane16 < 14, roll(v, -2), 0.0)

        def down_x(v):
            return jnp.where(lane16 >= 2, roll(v, 2), 0.0)

        for r in (0,) + chunks:
            a0, a1 = BL[j, r:r + 8, :], BL[j, r + 1:r + 9, :]
            b0, b1 = roll(BO[j, r:r + 8, :], -1), roll(BO[j, r + 1:r + 9, :], -1)
            c = BCL[r:r + 8, :]
            pushes = []
            s0, d0, s1, d1 = a0 + b0, b0 - a0, a1 + b1, b1 - a1
            fields = ((s0 + s1, 0), (s1 - s0, 1), (d0 + d1, 1), (d1 - d0, 2))
            outs = []
            for f, k in fields:
                g = up_x(f)
                td = (g - f) * (c * float(3 - k))
                ts = None if k == 0 else (f + g) * (c * float(4 - k))
                if ts is None:
                    outs.append(down_x(td) - td)
                else:
                    outs.append(ts - td + down_x(ts + td))
            ss, sd, ds, dd = outs
            ps, pd = ss + ds, sd + dd
            WC[0, r:r + 8, :] = ps + pd
            if r:
                push = ps - pd + WC[0, r - 1:r + 7, :]
                push = roll(push, 1)
            else:
                push = zero
            W[j, r:r + 8, :] = jnp.where(lax.rem(lane, 2) == 0, roll(BH[j, r:r + 8, :], -1), push)
        W[j, HI:RP, :] = roll(BH[j, HI:RP, :], -1)

    def step(j):
        scale = 2.0 if j else 1.0

        @pl.loop(0, L)
        def _(l):
            back = 128 - (16 * l + 1)
            acc_a, acc_b = zero, zero
            for r in (0,) + chunks:
                w0, w1 = W[j, r:r + 8, :], W[j, r + 1:r + 9, :]
                ws, wd = w0 + w1, w1 - w0
                b = zero
                carry = None
                last_f = None

                def node(x):
                    u0, u1 = U[j, l, x, r:r + 8, :], U[j, l, x, r + 1:r + 9, :]
                    amount = back - 2 * x
                    ys, yd = u0 + u1, u1 - u0
                    ns = jnp.where(lane == 127, roll(ws, amount), roll(ys, 127))
                    nd = jnp.where(lane == 127, roll(wd, amount), roll(yd, 127))
                    return (ys + ns, yd + nd, ns - ys, nd - yd)

                now = node(0)
                for x in range(X):
                    nxt = node(x + 1) if x + 1 < X else None
                    cs = (C1[x, r:r + 8, :], C2[x, r:r + 8, :], C3[x, r:r + 8, :])
                    outs, new_carry = [], []
                    for i, k in enumerate((0, 1, 1, 2)):
                        f = now[i]
                        if nxt is None:
                            d, s = -f, f
                        else:
                            d, s = nxt[i] - f, nxt[i] + f
                        td = d * cs[k]
                        if k == 0:
                            o, n = -td, td
                        else:
                            ts = s * cs[k - 1]
                            o, n = ts - td, ts + td
                        if carry is not None:
                            o = o + carry[i]
                        outs.append(o)
                        new_carry.append(n)
                    carry = new_carry
                    now = nxt
                    ss, sd, ds, dd = outs
                    PS[0, x, r:r + 8, :] = ss + sd
                    PS[1, x, r:r + 8, :] = ds + dd
                    if r == 0:
                        continue
                    q = r - LO
                    es = ss - sd + PS[0, x, r - 1:r + 7, :]
                    ed = ds - dd + PS[1, x, r - 1:r + 7, :]
                    push = jnp.where(lane == 0, roll(w0, back - 2 * x), roll(es + ed, 1))
                    image = es - ed + push
                    v = U[j, l, x, r:r + 8, :]
                    new = image * (INV[x, q:q + 8, :] * (scale / HALF)) - scale * v
                    if j:
                        new = new - U[j - 1, l, x, r:r + 8, :]
                    weighted = new * DIAG[x, q:q + 8, :]
                    acc_a = acc_a + v * weighted
                    if j + 1 < STEPS:
                        acc_b = acc_b + new * weighted
                        U[j + 1, l, x, r:r + 8, :] = new
                        b = jnp.where(lane16 >= 2 * x, roll(new, 16 * l + 2 * x + 1), b)
                        edges(j + 1, l, x, r, new)
                if r and j + 1 < STEPS:
                    pack_tail(j + 1, l, r, b)
            ACC[2 * j + 1, l] = acc_a
            if j + 1 < STEPS:
                ACC[2 * j + 2, l] = acc_b

    for j in range(STEPS):
        exchange(j, halo(j), False)
        fill(j)
        step(j)
        if j + 1 < STEPS:
            exchange(j + 1, halo(j + 1), True)

    rows = zero
    for k in range(2 * STEPS):
        for l in range(L):
            t = jnp.sum(jnp.sum(ACC[k, l], axis=0, keepdims=True), axis=1, keepdims=True)
            rows = jnp.where((sub == k) & (lane == l), t, rows)

    def spread(buffer, n, axis_z, base):
        def copy(d):
            target = (my_y, lax.rem(my_z + d, nz)) if axis_z else (lax.rem(my_y + d, ny), my_z)
            return pltpu.make_async_remote_copy(
                src_ref=buffer.at[0], dst_ref=buffer.at[d], send_sem=rsend.at[base + d],
                recv_sem=rrecv.at[base + d], device_id=target, device_id_type=MESH)
        for d in range(1, n):
            copy(d).start()
        for d in range(1, n):
            copy(d).wait()
        total = buffer[0]
        for d in range(1, n):
            total = total + buffer[d]
        return total

    AZ[0] = rows
    AY[0] = spread(AZ, nz, True, 0)
    RED[...] = spread(AY, ny, False, nz)
    a = [RED[k:k + 1, :] for k in range(2 * STEPS)]
    m = [a[0], a[1]]
    for k in range(2, 2 * STEPS):
        m.append(2.0 * a[k] - m[k % 2])

    def gram(i, j):
        return 0.5 * (m[i + j] + m[abs(i - j)])

    def times_m(c):
        out = [None] * (len(c) + 1)
        def put(i, v):
            out[i] = v if out[i] is None else out[i] + v
        for i, v in enumerate(c):
            put(i, HALF * v)
            put(i + 1, (HALF if i == 0 else 0.5 * HALF) * v)
            if i:
                put(i - 1, 0.5 * HALF * v)
        return out

    def form(c, e):
        total = 0.0
        for i, v in enumerate(c):
            for k, w in enumerate(e):
                total = total + v * w * gram(i, k)
        return total

    one = jnp.ones((1, Z), f32)
    zc, dc, tc = [one], [one], []
    rz = form(zc, zc)
    for it in range(STEPS):
        image = times_m(dc)
        alpha = rz / form(dc, image)
        tc = [alpha * v + (tc[i] if i < len(tc) else 0.0) for i, v in enumerate(dc)]
        if it + 1 == STEPS:
            break
        zc = [(zc[i] if i < len(zc) else 0.0) - alpha * v for i, v in enumerate(image)]
        new = form(zc, zc)
        beta = new / rz
        dc = [v + (beta * dc[i] if i < len(dc) else 0.0) for i, v in enumerate(zc)]
        rz = new

    packed = [zero] * STEPS
    for i in range(STEPS):
        for l in range(L):
            t = jnp.sum(jnp.where(lane[0:1] == l, tc[i], 0.0), axis=1, keepdims=True)
            t = jnp.broadcast_to(t, (8, Z))
            COEF[i, l] = t
            packed[i] = jnp.where(group == l, t, packed[i])
    for r in chunks + (HI,):
        WC[0, r:r + 8, :] = sum(packed[i] * W[i, r:r + 8, :] for i in range(1, STEPS)) + packed[0] * W[0, r:r + 8, :]

    S[...] = jnp.zeros(S.shape, f32)

    @pl.loop(0, L)
    def _(l):
        cs = [COEF[i, l] for i in range(STEPS)]
        back = 128 - (16 * l + 1)
        for x in range(X):
            for r in chunks + (HI,):
                t = cs[0] * U[0, l, x, r:r + 8, :]
                for i in range(1, STEPS):
                    t = t + cs[i] * U[i, l, x, r:r + 8, :]
                PS[0, x, r:r + 8, :] = t
                if r < HI:
                    temp[l, x, r - LO:r - LO + 8, :] = t
        for r in chunks:
            w0, w1 = WC[0, r:r + 8, :], WC[0, r + 1:r + 9, :]
            ws, wd = w0 + w1, w1 - w0

            def node(x):
                u0, u1 = PS[0, x, r:r + 8, :], PS[0, x, r + 1:r + 9, :]
                amount = back - 2 * x
                ys, yd = u0 + u1, u1 - u0
                ns = jnp.where(lane == 127, roll(ws, amount), roll(ys, 127))
                nd = jnp.where(lane == 127, roll(wd, amount), roll(yd, 127))
                return (ys + ns, yd + nd, ns - ys, nd - yd)

            now = node(0)
            for x in range(X):
                nxt = node(x + 1) if x + 1 < X else (zero,) * 4
                groups = [None, None, None]
                for i, k in enumerate((0, 1, 1, 2)):
                    d = nxt[i] - now[i]
                    groups[k] = d * d if groups[k] is None else groups[k] + d * d
                    if k:
                        s = nxt[i] + now[i]
                        groups[k - 1] = groups[k - 1] + s * s
                now = nxt
                S[x, r:r + 8, :] += 3.0 * groups[0] + 2.0 * groups[1] + groups[2]

    def mass(index, total):
        out = jnp.zeros(index.shape, f32)
        for s in range(-3, 4):
            ok = (index + s >= 0) & (index + s < total)
            out = out + jnp.where(ok, 4.0 - abs(s), 0.0)
        return out

    mz = mass(my_z * Z + lane, nz * Z)
    for r in chunks:
        my = mass(my_y * R + (r - LO) + sub, ny * R)
        inv_yz = (-3.0 * (1.0 - FLOOR) / (48.0 * L)) / (my * mz)
        vs = []
        for x in range(X):
            density = (seed[x, r - LO:r - LO + 8, :].astype(f32) + 1.0) / 16.0
            mx = float(sum(4 - abs(s) for s in range(-3, 4) if 0 <= x + s < X))
            vs.append(S[x, r:r + 8, :] * (density * density) * inv_yz * (1.0 / mx))
        b = zero
        for x in range(X):
            v = 4.0 * vs[x]
            for s in (1, 2, 3):
                for o in (x - s, x + s):
                    if 0 <= o < X:
                        v = v + (4.0 - s) * vs[o]
            S[x, r:r + 8, :] = v
            b = jnp.where(lane >= 16 * x, roll(v, 16 * x + 8), b)
        PZ[r - LO:r - LO + 8, :] = b

    top, bottom = pl.ds(R - 8, 8), pl.ds(0, 8)
    final = (
        (1, 0, S.at[:, last], SLO), (-1, 0, S.at[:, first], SHI),
        (0, 1, PZ, PZL.at[mid]), (0, -1, PZ, PZH.at[mid]),
        (1, 1, PZ.at[top], PZL.at[low]), (1, -1, PZ.at[top], PZH.at[low]),
        (-1, 1, PZ.at[bottom], PZL.at[high]), (-1, -1, PZ.at[bottom], PZH.at[high]),
    )
    exchange(STEPS + 1, final, True)
    exchange(STEPS + 1, final, False)
    for x in range(X):
        S[x, 0:LO, :] = SLO[x]
        S[x, HI:RP, :] = SHI[x]
    for r in (0,) + chunks + (HI,):
        PM[r:r + 8, :] = jnp.where(lane16 < 8, PZL[r:r + 8, :], PZH[r:r + 8, :])

    def along_y(get):
        v = 4.0 * get(0)
        for s in (1, 2, 3):
            v = v + (4.0 - s) * (get(s) + get(-s))
        return v

    for r in chunks:
        pm = along_y(lambda s: PM[r + s:r + s + 8, :])
        for x in range(X):
            v = along_y(lambda s: S[x, r + s:r + s + 8, :])
            w = roll(pm, -(16 * x + 8))
            out = 4.0 * v
            for s in (1, 2, 3):
                up = jnp.where(lane >= 128 - s, roll(w, -s), roll(v, -s))
                down = jnp.where(lane < s, roll(w, s), roll(v, s))
                out = out + (4.0 - s) * (up + down)
            sens[x, r - LO:r - LO + 8, :] = out


def on_device(ny, nz, seed, heat, source, fixed):
    f32 = jnp.float32
    v = pltpu.VMEM
    scratch = [
        v((STEPS, L, X, RP, Z), f32),
        v((STEPS, RP, Z), f32), v((STEPS, RP, Z), f32), v((STEPS, RP, Z), f32),
        v((STEPS, L, X, Z), f32), v((STEPS, L, X, Z), f32),
        v((STEPS, L, X, Z), f32), v((STEPS, L, X, Z), f32),
        v((STEPS, RP, Z), f32), v((1, RP, Z), f32),
        v((X, RP, Z), f32), v((X, RP, Z), f32), v((X, RP, Z), f32),
        v((X, R, Z), f32), v((X, R, Z), f32),
        v((2, X, RP, Z), f32),
        v((2 * STEPS, L, 8, Z), f32), v((8, Z), f32), v((STEPS, L, 8, Z), f32),
        v((R, Z), f32), v((RP, Z), f32), v((X, Z), f32), v((X, Z), f32),
        v((X, RP, Z), f32), v((X, 8, Z), f32), v((X, 8, Z), f32),
        v((R, Z), f32), v((RP, Z), f32), v((RP, Z), f32), v((RP, Z), f32),
        v((nz, 8, Z), f32), v((ny, 8, Z), f32),
        pltpu.SemaphoreType.DMA((STEPS + 2, 10)), pltpu.SemaphoreType.DMA((STEPS + 2, 10)),
        pltpu.SemaphoreType.DMA((ny + nz,)), pltpu.SemaphoreType.DMA((ny + nz,)),
    ]
    return pl.pallas_call(
        functools.partial(kernel, ny, nz),
        out_shape=(jax.ShapeDtypeStruct((L, X, R, Z), f32), jax.ShapeDtypeStruct((X, R, Z), f32)),
        in_specs=[pl.BlockSpec(memory_space=pltpu.VMEM)] * 4,
        out_specs=(pl.BlockSpec(memory_space=pltpu.VMEM),) * 2,
        scratch_shapes=scratch,
        compiler_params=pltpu.CompilerParams(
            collective_id=0, has_side_effects=True, vmem_limit_bytes=40 * 2**20
        ),
    )(seed, heat, source, fixed)


def solution(mesh):
    in_specs = (
        P(None, "gy", "gz"),
        P(None, None, "gy", "gz"),
        P(None, "gy", "gz"),
        P(None, "gy", "gz"),
    )
    out_specs = (P(None, None, "gy", "gz"), P(None, "gy", "gz"))
    body = functools.partial(on_device, mesh.shape["gy"], mesh.shape["gz"])
    return jax.shard_map(body, mesh=mesh, in_specs=in_specs, out_specs=out_specs, check_vma=False)
```

```python
import functools

import jax
import jax.numpy as jnp
from jax import lax
from jax.experimental import pallas as pl
from jax.experimental.pallas import tpu as pltpu
from jax.sharding import PartitionSpec as P

STEPS = 4
L, X = 8, 8
R, Z = 64, 128
LO, HI, RP = 8, 72, 80
MESH = pl.DeviceIdType.MESH
FLOOR = 0.01
HALF = 0.75

NEAR = ((1, 0), (-1, 0), (0, 1), (0, -1), (1, 1), (1, -1), (-1, 1), (-1, -1))


def roll(v, shift):
    if isinstance(shift, int):
        shift = shift % 128
        if shift == 0:
            return v
    return pltpu.roll(v, shift, v.ndim - 1)


def kernel(ny, nz, seed, heat, source, fixed, temp, sens,
           U0, U1, U2, U3, BL, BO, BH, ELO, EHI, ETOP, EBOT, W, WC,
           C1, C2, C3, INV, DIAG, PS, ACC, RED, COEF,
           BC, BCL, CTOP, CLO, S, SLO, SHI, PZ, PZL, PZH, PM,
           AZ, AY, send, recv, rsend, rrecv):
    my_y, my_z = lax.axis_index("gy"), lax.axis_index("gz")
    f32 = jnp.float32
    U = (U0, U1, U2, U3)
    lane = lax.broadcasted_iota(jnp.int32, (8, Z), 1)
    sub = lax.broadcasted_iota(jnp.int32, (8, Z), 0)
    lane16 = lax.rem(lane, 16)
    group = lax.div(lane, 16)
    zero = jnp.zeros((8, Z), f32)
    chunks = tuple(range(LO, HI, 8))

    def inside(dy, dz):
        ok = None
        for d, me, n in ((dy, my_y, ny), (dz, my_z, nz)):
            if d:
                this = (me + d >= 0) & (me + d < n)
                ok = this if ok is None else ok & this
        return ok

    for ref in (BL, BO, BH):
        ref[...] = jnp.zeros(ref.shape, f32)
    for ref in (ELO, EHI, BCL, CLO, SLO, SHI, PZL, PZH, C1, C2, C3, W):
        ref[...] = jnp.zeros(ref.shape, f32)

    barrier = pltpu.get_barrier_semaphore()
    for d in range(1, nz):
        pl.semaphore_signal(barrier, inc=1, device_id=(my_y, lax.rem(my_z + d, nz)), device_id_type=MESH)
    for d in range(1, ny):
        pl.semaphore_signal(barrier, inc=1, device_id=(lax.rem(my_y + d, ny), my_z), device_id_type=MESH)
    for dy, dz in NEAR[4:]:
        @pl.when(inside(dy, dz))
        def _(dy=dy, dz=dz):
            pl.semaphore_signal(barrier, inc=1, device_id=(my_y + dy, my_z + dz), device_id_type=MESH)

    for x in range(X):
        for r in range(0, R, 8):
            density = (seed[x, r:r + 8, :].astype(f32) + 1.0) / 16.0
            cond = (FLOOR + (1.0 - FLOOR) * (density * density * density)) * (1.0 / 48.0)
            C1[x, LO + r:LO + r + 8, :] = cond * 3.0
            C2[x, LO + r:LO + r + 8, :] = cond * 2.0
            C3[x, LO + r:LO + r + 8, :] = cond
            if r == R - 8:
                CTOP[x:x + 1, :] = cond[7:8, :]
    for r in range(LO, HI, 8):
        b = zero
        for x in range(X):
            b = jnp.where(lane16 >= 2 * x, roll(C3[x, r:r + 8, :], 2 * x + 1), b)
        b = jnp.where(group == 0, b, 0.0)
        for s in (16, 32, 64):
            b = b + roll(b, s)
        BC[r - LO:r - LO + 8, :] = b

    def sides(me, n):
        return jnp.where(me > 0, 1, 0) + jnp.where(me + 1 < n, 1, 0)

    pl.semaphore_wait(barrier, nz - 1 + ny - 1 + sides(my_y, ny) * sides(my_z, nz))

    def exchange(e, messages, start):
        for i, (dy, dz, src, dst) in enumerate(messages):
            def copy(dy=dy, dz=dz, src=src, dst=dst, i=i):
                return pltpu.make_async_remote_copy(
                    src_ref=src, dst_ref=dst, send_sem=send.at[e, i], recv_sem=recv.at[e, i],
                    device_id=(my_y + dy, my_z + dz), device_id_type=MESH)
            if start:
                @pl.when(inside(dy, dz))
                def _(copy=copy):
                    copy().start()
            else:
                @pl.when(inside(dy, dz))
                def _(copy=copy):
                    copy().wait_send()
                @pl.when(inside(-dy, -dz))
                def _(copy=copy):
                    copy().wait_recv()

    low, high = pl.ds(0, 8), pl.ds(HI, 8)
    first, last, mid = pl.ds(LO, 8), pl.ds(HI - 8, 8), pl.ds(LO, R)

    def halo(j):
        own = BO.at[j]
        return (
            (1, 0, ETOP.at[j], ELO.at[j]), (-1, 0, EBOT.at[j], EHI.at[j]),
            (0, 1, own.at[mid], BL.at[j].at[mid]), (0, -1, own.at[mid], BH.at[j].at[mid]),
            (1, 0, own.at[last], BO.at[j].at[low]), (-1, 0, own.at[first], BO.at[j].at[high]),
            (1, 1, own.at[last], BL.at[j].at[low]), (1, -1, own.at[last], BH.at[j].at[low]),
            (-1, 1, own.at[first], BL.at[j].at[high]), (-1, -1, own.at[first], BH.at[j].at[high]),
        )

    cond_messages = (
        (1, 0, CTOP, CLO),
        (0, 1, BC, BCL.at[mid]),
        (1, 1, BC.at[pl.ds(R - 8, 8)], BCL.at[low]),
    )
    exchange(STEPS, cond_messages, True)
    exchange(STEPS, cond_messages, False)
    for x in range(X):
        for ref, k in ((C1, 3.0), (C2, 2.0), (C3, 1.0)):
            ref[x, LO - 1:LO, :] = CLO[x:x + 1, :] * k

    for r in chunks:
        low_z = BCL[r:r + 8, :] + BCL[r - 1:r + 7, :]
        low_z = low_z + jnp.where(lane16 >= 2, roll(low_z, 2), 0.0)
        before = None
        for x in range(X):
            t = C3[x, r:r + 8, :] + C3[x, r - 1:r + 7, :]
            both = t if before is None else t + before
            before = t
            below = jnp.where(lane == 0, roll(low_z, -2 * x), roll(both, 1))
            total = (both + below) * 48.0 / 3.0
            free = 1.0 - fixed[x, r - LO:r - LO + 8, :].astype(f32)
            DIAG[x, r - LO:r - LO + 8, :] = total
            INV[x, r - LO:r - LO + 8, :] = free / total

    def pack_tail(j, l, r, b):
        BO[j, r:r + 8, :] = jnp.where(group == l, b, BO[j, r:r + 8, :])

    def edges(j, l, x, r, v):
        if r == LO:
            EBOT[j, l, x:x + 1, :] = v[0:1, :]
        if r == HI - 8:
            ETOP[j, l, x:x + 1, :] = v[7:8, :]

    @pl.loop(0, L)
    def _(l):
        acc = zero
        for r in chunks:
            b = zero
            q = r - LO
            for x in range(X):
                inv = INV[x, q:q + 8, :]
                rhs = heat[l, x, q:q + 8, :] * source[x, q:q + 8, :].astype(f32)
                v = rhs * inv
                U[0][l, x, r:r + 8, :] = v
                acc = acc + v * v * DIAG[x, q:q + 8, :]
                b = jnp.where(lane16 >= 2 * x, roll(v, 16 * l + 2 * x + 1), b)
                edges(0, l, x, r, v)
            pack_tail(0, l, r, b)
        ACC[0, l] = acc
    exchange(0, halo(0), True)

    def fill(j):
        @pl.loop(0, L)
        def _(l):
            for x in range(X):
                U[j][l, x, LO - 1:LO, :] = ELO[j, l, x:x + 1, :]
                U[j][l, x, HI:HI + 1, :] = EHI[j, l, x:x + 1, :]

        def up_x(v):
            return jnp.where(lane16 < 14, roll(v, -2), 0.0)

        def down_x(v):
            return jnp.where(lane16 >= 2, roll(v, 2), 0.0)

        for r in (0,) + chunks:
            a0, a1 = BL[j, r:r + 8, :], BL[j, r + 1:r + 9, :]
            b0, b1 = roll(BO[j, r:r + 8, :], -1), roll(BO[j, r + 1:r + 9, :], -1)
            c = BCL[r:r + 8, :]
            pushes = []
            s0, d0, s1, d1 = a0 + b0, b0 - a0, a1 + b1, b1 - a1
            fields = ((s0 + s1, 0), (s1 - s0, 1), (d0 + d1, 1), (d1 - d0, 2))
            outs = []
            for f, k in fields:
                g = up_x(f)
                td = (g - f) * (c * float(3 - k))
                ts = None if k == 0 else (f + g) * (c * float(4 - k))
                if ts is None:
                    outs.append(down_x(td) - td)
                else:
                    outs.append(ts - td + down_x(ts + td))
            ss, sd, ds, dd = outs
            ps, pd = ss + ds, sd + dd
            WC[0, r:r + 8, :] = ps + pd
            if r:
                push = ps - pd + WC[0, r - 1:r + 7, :]
                push = roll(push, 1)
            else:
                push = zero
            W[j, r:r + 8, :] = jnp.where(lax.rem(lane, 2) == 0, roll(BH[j, r:r + 8, :], -1), push)
        W[j, HI:RP, :] = roll(BH[j, HI:RP, :], -1)

    def next_row(v, following):
        return pltpu.roll(jnp.where(sub == 0, following, v), 7, 0)

    def step(j):
        scale = 2.0 if j else 1.0

        @pl.loop(0, L)
        def _(l):
            back = 128 - (16 * l + 1)
            def chunk(r, above, sums):
                here, ahead = pl.ds(r, 8), pl.ds(r + 8, 8)
                if sums is not None:
                    here, ahead = pl.ds(pl.multiple_of(r, 8), 8), pl.ds(pl.multiple_of(r + 8, 8), 8)
                    owned = pl.ds(pl.multiple_of(r - LO, 8), 8)
                    acc_a, acc_b = sums
                w0 = W[j, here, :]
                w1 = next_row(w0, W[j, ahead, :])
                ws, wd = w0 + w1, w1 - w0

                def node(x):
                    u0 = U[j][l, x, here, :]
                    u1 = next_row(u0, U[j][l, x, ahead, :])
                    amount = back - 2 * x
                    ys, yd = u0 + u1, u1 - u0
                    ns = jnp.where(lane == 127, roll(ws, amount), roll(ys, 127))
                    nd = jnp.where(lane == 127, roll(wd, amount), roll(yd, 127))
                    return (ys + ns, yd + nd, ns - ys, nd - yd)

                now, carry, b = node(0), None, zero
                pushed, news = [], []
                for x in range(X):
                    nxt = node(x + 1) if x + 1 < X else None
                    cs = (C1[x, here, :], C2[x, here, :], C3[x, here, :])
                    outs, new_carry = [], []
                    for i, k in enumerate((0, 1, 1, 2)):
                        f = now[i]
                        if nxt is None:
                            d, s = -f, f
                        else:
                            d, s = nxt[i] - f, nxt[i] + f
                        td = d * cs[k]
                        if k == 0:
                            o, n = -td, td
                        else:
                            ts = s * cs[k - 1]
                            o, n = ts - td, ts + td
                        if carry is not None:
                            o = o + carry[i]
                        outs.append(o)
                        new_carry.append(n)
                    carry = new_carry
                    now = nxt
                    ss, sd, ds, dd = outs
                    ps, pd = ss + sd, ds + dd
                    pushed += [ps, pd]
                    if sums is None:
                        continue
                    es = ss - sd + pltpu.roll(jnp.where(sub == 7, above[2 * x], ps), 1, 0)
                    ed = ds - dd + pltpu.roll(jnp.where(sub == 7, above[2 * x + 1], pd), 1, 0)
                    push = jnp.where(lane == 0, roll(w0, back - 2 * x), roll(es + ed, 1))
                    image = es - ed + push
                    v = U[j][l, x, here, :]
                    new = image * (INV[x, owned, :] * (scale / HALF)) - scale * v
                    if j:
                        new = new - U[j - 1][l, x, here, :]
                    weighted = new * DIAG[x, owned, :]
                    acc_a = acc_a + v * weighted
                    if j + 1 < STEPS:
                        acc_b = acc_b + new * weighted
                        b = jnp.where(lane16 >= 2 * x, roll(new, 16 * l + 2 * x + 1), b)
                        news.append(new)
                if news:
                    for x, new in enumerate(news):
                        U[j + 1][l, x, here, :] = new
                    BO[j + 1, here, :] = jnp.where(group == l, b, BO[j + 1, here, :])
                if sums is None:
                    return tuple(pushed)
                return tuple(pushed), (acc_a, acc_b)

            _, (acc_a, acc_b) = lax.fori_loop(
                1, HI // 8, lambda c, carry: chunk(c * 8, *carry), (chunk(0, None, None), (zero, zero)))
            ACC[2 * j + 1, l] = acc_a
            if j + 1 < STEPS:
                ACC[2 * j + 2, l] = acc_b
                for x in range(X):
                    EBOT[j + 1, l, x:x + 1, :] = U[j + 1][l, x, LO:LO + 1, :]
                    ETOP[j + 1, l, x:x + 1, :] = U[j + 1][l, x, HI - 1:HI, :]

    for j in range(STEPS):
        exchange(j, halo(j), False)
        fill(j)
        step(j)
        if j + 1 < STEPS:
            exchange(j + 1, halo(j + 1), True)

    rows = zero
    for k in range(2 * STEPS):
        for l in range(L):
            t = jnp.sum(jnp.sum(ACC[k, l], axis=0, keepdims=True), axis=1, keepdims=True)
            rows = jnp.where((sub == k) & (lane == l), t, rows)

    def spread(buffer, n, axis_z, base):
        def copy(d):
            target = (my_y, lax.rem(my_z + d, nz)) if axis_z else (lax.rem(my_y + d, ny), my_z)
            return pltpu.make_async_remote_copy(
                src_ref=buffer.at[0], dst_ref=buffer.at[d], send_sem=rsend.at[base + d],
                recv_sem=rrecv.at[base + d], device_id=target, device_id_type=MESH)
        for d in range(1, n):
            copy(d).start()
        for d in range(1, n):
            copy(d).wait()
        total = buffer[0]
        for d in range(1, n):
            total = total + buffer[d]
        return total

    AZ[0] = rows
    AY[0] = spread(AZ, nz, True, 0)
    RED[...] = spread(AY, ny, False, nz)
    a = [RED[k:k + 1, :] for k in range(2 * STEPS)]
    m = [a[0], a[1]]
    for k in range(2, 2 * STEPS):
        m.append(2.0 * a[k] - m[k % 2])

    def gram(i, j):
        return 0.5 * (m[i + j] + m[abs(i - j)])

    def times_m(c):
        out = [None] * (len(c) + 1)
        def put(i, v):
            out[i] = v if out[i] is None else out[i] + v
        for i, v in enumerate(c):
            put(i, HALF * v)
            put(i + 1, (HALF if i == 0 else 0.5 * HALF) * v)
            if i:
                put(i - 1, 0.5 * HALF * v)
        return out

    def form(c, e):
        total = 0.0
        for i, v in enumerate(c):
            for k, w in enumerate(e):
                total = total + v * w * gram(i, k)
        return total

    one = jnp.ones((1, Z), f32)
    zc, dc, tc = [one], [one], []
    rz = form(zc, zc)
    for it in range(STEPS):
        image = times_m(dc)
        alpha = rz / form(dc, image)
        tc = [alpha * v + (tc[i] if i < len(tc) else 0.0) for i, v in enumerate(dc)]
        if it + 1 == STEPS:
            break
        zc = [(zc[i] if i < len(zc) else 0.0) - alpha * v for i, v in enumerate(image)]
        new = form(zc, zc)
        beta = new / rz
        dc = [v + (beta * dc[i] if i < len(dc) else 0.0) for i, v in enumerate(zc)]
        rz = new

    packed = [zero] * STEPS
    for i in range(STEPS):
        for l in range(L):
            t = jnp.sum(jnp.where(lane[0:1] == l, tc[i], 0.0), axis=1, keepdims=True)
            t = jnp.broadcast_to(t, (8, Z))
            COEF[i, l] = t
            packed[i] = jnp.where(group == l, t, packed[i])
    for r in chunks + (HI,):
        WC[0, r:r + 8, :] = sum(packed[i] * W[i, r:r + 8, :] for i in range(1, STEPS)) + packed[0] * W[0, r:r + 8, :]

    S[...] = jnp.zeros(S.shape, f32)

    @pl.loop(0, L)
    def _(l):
        cs = [COEF[i, l] for i in range(STEPS)]
        back = 128 - (16 * l + 1)
        for x in range(X):
            for r in chunks + (HI,):
                t = cs[0] * U[0][l, x, r:r + 8, :]
                for i in range(1, STEPS):
                    t = t + cs[i] * U[i][l, x, r:r + 8, :]
                PS[0, x, r:r + 8, :] = t
                if r < HI:
                    temp[l, x, r - LO:r - LO + 8, :] = t
        for r in chunks:
            w0, w1 = WC[0, r:r + 8, :], WC[0, r + 1:r + 9, :]
            ws, wd = w0 + w1, w1 - w0

            def node(x):
                u0, u1 = PS[0, x, r:r + 8, :], PS[0, x, r + 1:r + 9, :]
                amount = back - 2 * x
                ys, yd = u0 + u1, u1 - u0
                ns = jnp.where(lane == 127, roll(ws, amount), roll(ys, 127))
                nd = jnp.where(lane == 127, roll(wd, amount), roll(yd, 127))
                return (ys + ns, yd + nd, ns - ys, nd - yd)

            now = node(0)
            for x in range(X):
                nxt = node(x + 1) if x + 1 < X else (zero,) * 4
                groups = [None, None, None]
                for i, k in enumerate((0, 1, 1, 2)):
                    d = nxt[i] - now[i]
                    groups[k] = d * d if groups[k] is None else groups[k] + d * d
                    if k:
                        s = nxt[i] + now[i]
                        groups[k - 1] = groups[k - 1] + s * s
                now = nxt
                S[x, r:r + 8, :] += 3.0 * groups[0] + 2.0 * groups[1] + groups[2]

    def mass(index, total):
        out = jnp.zeros(index.shape, f32)
        for s in range(-3, 4):
            ok = (index + s >= 0) & (index + s < total)
            out = out + jnp.where(ok, 4.0 - abs(s), 0.0)
        return out

    mz = mass(my_z * Z + lane, nz * Z)
    for r in chunks:
        my = mass(my_y * R + (r - LO) + sub, ny * R)
        inv_yz = (-3.0 * (1.0 - FLOOR) / (48.0 * L)) / (my * mz)
        vs = []
        for x in range(X):
            density = (seed[x, r - LO:r - LO + 8, :].astype(f32) + 1.0) / 16.0
            mx = float(sum(4 - abs(s) for s in range(-3, 4) if 0 <= x + s < X))
            vs.append(S[x, r:r + 8, :] * (density * density) * inv_yz * (1.0 / mx))
        b = zero
        for x in range(X):
            v = 4.0 * vs[x]
            for s in (1, 2, 3):
                for o in (x - s, x + s):
                    if 0 <= o < X:
                        v = v + (4.0 - s) * vs[o]
            S[x, r:r + 8, :] = v
            b = jnp.where(lane >= 16 * x, roll(v, 16 * x + 8), b)
        PZ[r - LO:r - LO + 8, :] = b

    top, bottom = pl.ds(R - 8, 8), pl.ds(0, 8)
    final = (
        (1, 0, S.at[:, last], SLO), (-1, 0, S.at[:, first], SHI),
        (0, 1, PZ, PZL.at[mid]), (0, -1, PZ, PZH.at[mid]),
        (1, 1, PZ.at[top], PZL.at[low]), (1, -1, PZ.at[top], PZH.at[low]),
        (-1, 1, PZ.at[bottom], PZL.at[high]), (-1, -1, PZ.at[bottom], PZH.at[high]),
    )
    exchange(STEPS + 1, final, True)
    exchange(STEPS + 1, final, False)
    for x in range(X):
        S[x, 0:LO, :] = SLO[x]
        S[x, HI:RP, :] = SHI[x]
    for r in (0,) + chunks + (HI,):
        PM[r:r + 8, :] = jnp.where(lane16 < 8, PZL[r:r + 8, :], PZH[r:r + 8, :])

    def along_y(get):
        v = 4.0 * get(0)
        for s in (1, 2, 3):
            v = v + (4.0 - s) * (get(s) + get(-s))
        return v

    for r in chunks:
        pm = along_y(lambda s: PM[r + s:r + s + 8, :])
        for x in range(X):
            v = along_y(lambda s: S[x, r + s:r + s + 8, :])
            w = roll(pm, -(16 * x + 8))
            out = 4.0 * v
            for s in (1, 2, 3):
                up = jnp.where(lane >= 128 - s, roll(w, -s), roll(v, -s))
                down = jnp.where(lane < s, roll(w, s), roll(v, s))
                out = out + (4.0 - s) * (up + down)
            sens[x, r - LO:r - LO + 8, :] = out


def on_device(ny, nz, seed, heat, source, fixed):
    f32 = jnp.float32
    v = pltpu.VMEM
    scratch = [
        *(v((L, X, RP, Z), f32) for _ in range(STEPS)),
        v((STEPS, RP, Z), f32), v((STEPS, RP, Z), f32), v((STEPS, RP, Z), f32),
        v((STEPS, L, X, Z), f32), v((STEPS, L, X, Z), f32),
        v((STEPS, L, X, Z), f32), v((STEPS, L, X, Z), f32),
        v((STEPS, RP, Z), f32), v((1, RP, Z), f32),
        v((X, RP, Z), f32), v((X, RP, Z), f32), v((X, RP, Z), f32),
        v((X, R, Z), f32), v((X, R, Z), f32),
        v((1, X, RP, Z), f32),
        v((2 * STEPS, L, 8, Z), f32), v((8, Z), f32), v((STEPS, L, 8, Z), f32),
        v((R, Z), f32), v((RP, Z), f32), v((X, Z), f32), v((X, Z), f32),
        v((X, RP, Z), f32), v((X, 8, Z), f32), v((X, 8, Z), f32),
        v((R, Z), f32), v((RP, Z), f32), v((RP, Z), f32), v((RP, Z), f32),
        v((nz, 8, Z), f32), v((ny, 8, Z), f32),
        pltpu.SemaphoreType.DMA((STEPS + 2, 10)), pltpu.SemaphoreType.DMA((STEPS + 2, 10)),
        pltpu.SemaphoreType.DMA((ny + nz,)), pltpu.SemaphoreType.DMA((ny + nz,)),
    ]
    return pl.pallas_call(
        functools.partial(kernel, ny, nz),
        out_shape=(jax.ShapeDtypeStruct((L, X, R, Z), f32), jax.ShapeDtypeStruct((X, R, Z), f32)),
        in_specs=[pl.BlockSpec(memory_space=pltpu.VMEM)] * 4,
        out_specs=(pl.BlockSpec(memory_space=pltpu.VMEM),) * 2,
        scratch_shapes=scratch,
        compiler_params=pltpu.CompilerParams(
            collective_id=0, has_side_effects=True, vmem_limit_bytes=40 * 2**20
        ),
    )(seed, heat, source, fixed)


def solution(mesh):
    in_specs = (
        P(None, "gy", "gz"),
        P(None, None, "gy", "gz"),
        P(None, "gy", "gz"),
        P(None, "gy", "gz"),
    )
    out_specs = (P(None, None, "gy", "gz"), P(None, "gy", "gz"))
    body = functools.partial(on_device, mesh.shape["gy"], mesh.shape["gz"])
    return jax.shard_map(body, mesh=mesh, in_specs=in_specs, out_specs=out_specs, check_vma=False)
```

```python
import functools

import jax
import jax.numpy as jnp
from jax import lax
from jax.experimental import pallas as pl
from jax.experimental.pallas import tpu as pltpu
from jax.sharding import PartitionSpec as P

STEPS = 4
L, X = 8, 8
R, Z = 64, 128
LO, HI, RP = 8, 72, 80
MESH = pl.DeviceIdType.MESH
FLOOR = 0.01
HALF = 0.75

NEAR = ((1, 0), (-1, 0), (0, 1), (0, -1), (1, 1), (1, -1), (-1, 1), (-1, -1))


def roll(v, shift):
    if isinstance(shift, int):
        shift = shift % 128
        if shift == 0:
            return v
    return pltpu.roll(v, shift, v.ndim - 1)


def kernel(ny, nz, seed, heat, source, fixed, temp, sens,
           U0, U1, U2, U3, BL, BO, BH, ELO, EHI, ETOP, EBOT, W, WC,
           C1, C2, C3, INV, DIAG, PS, ACC, RED, COEF,
           BC, BCL, CTOP, CLO, S, SLO, SHI, PZ, PZL, PZH, PM,
           AZ, AY, send, recv, rsend, rrecv):
    my_y, my_z = lax.axis_index("gy"), lax.axis_index("gz")
    f32 = jnp.float32
    U = (U0, U1, U2, U3)
    lane = lax.broadcasted_iota(jnp.int32, (8, Z), 1)
    sub = lax.broadcasted_iota(jnp.int32, (8, Z), 0)
    lane16 = lax.rem(lane, 16)
    group = lax.div(lane, 16)
    zero = jnp.zeros((8, Z), f32)
    chunks = tuple(range(LO, HI, 8))

    def inside(dy, dz):
        ok = None
        for d, me, n in ((dy, my_y, ny), (dz, my_z, nz)):
            if d:
                this = (me + d >= 0) & (me + d < n)
                ok = this if ok is None else ok & this
        return ok

    for ref in (BL, BO, BH):
        ref[...] = jnp.zeros(ref.shape, f32)
    for ref in (ELO, EHI, BCL, CLO, SLO, SHI, PZL, PZH, C1, C2, C3, W):
        ref[...] = jnp.zeros(ref.shape, f32)

    barrier = pltpu.get_barrier_semaphore()
    for d in range(1, nz):
        pl.semaphore_signal(barrier, inc=1, device_id=(my_y, lax.rem(my_z + d, nz)), device_id_type=MESH)
    for d in range(1, ny):
        pl.semaphore_signal(barrier, inc=1, device_id=(lax.rem(my_y + d, ny), my_z), device_id_type=MESH)
    for dy, dz in NEAR[4:]:
        @pl.when(inside(dy, dz))
        def _(dy=dy, dz=dz):
            pl.semaphore_signal(barrier, inc=1, device_id=(my_y + dy, my_z + dz), device_id_type=MESH)

    for x in range(X):
        for r in range(0, R, 8):
            density = (seed[x, r:r + 8, :].astype(f32) + 1.0) / 16.0
            cond = (FLOOR + (1.0 - FLOOR) * (density * density * density)) * (1.0 / 48.0)
            C1[x, LO + r:LO + r + 8, :] = cond * 3.0
            C2[x, LO + r:LO + r + 8, :] = cond * 2.0
            C3[x, LO + r:LO + r + 8, :] = cond
            if r == R - 8:
                CTOP[x:x + 1, :] = cond[7:8, :]
    for r in range(LO, HI, 8):
        b = zero
        for x in range(X):
            b = jnp.where(lane16 >= 2 * x, roll(C3[x, r:r + 8, :], 2 * x + 1), b)
        b = jnp.where(group == 0, b, 0.0)
        for s in (16, 32, 64):
            b = b + roll(b, s)
        BC[r - LO:r - LO + 8, :] = b

    def sides(me, n):
        return jnp.where(me > 0, 1, 0) + jnp.where(me + 1 < n, 1, 0)

    pl.semaphore_wait(barrier, nz - 1 + ny - 1 + sides(my_y, ny) * sides(my_z, nz))

    def exchange(e, messages, start):
        for i, (dy, dz, src, dst) in enumerate(messages):
            def copy(dy=dy, dz=dz, src=src, dst=dst, i=i):
                return pltpu.make_async_remote_copy(
                    src_ref=src, dst_ref=dst, send_sem=send.at[e, i], recv_sem=recv.at[e, i],
                    device_id=(my_y + dy, my_z + dz), device_id_type=MESH)
            if start:
                @pl.when(inside(dy, dz))
                def _(copy=copy):
                    copy().start()
            else:
                @pl.when(inside(dy, dz))
                def _(copy=copy):
                    copy().wait_send()
                @pl.when(inside(-dy, -dz))
                def _(copy=copy):
                    copy().wait_recv()

    low, high = pl.ds(0, 8), pl.ds(HI, 8)
    first, last, mid = pl.ds(LO, 8), pl.ds(HI - 8, 8), pl.ds(LO, R)

    def halo(j):
        own = BO.at[j]
        return (
            (1, 0, ETOP.at[j], ELO.at[j]), (-1, 0, EBOT.at[j], EHI.at[j]),
            (0, 1, own.at[mid], BL.at[j].at[mid]), (0, -1, own.at[mid], BH.at[j].at[mid]),
            (1, 0, own.at[last], BO.at[j].at[low]), (-1, 0, own.at[first], BO.at[j].at[high]),
            (1, 1, own.at[last], BL.at[j].at[low]), (1, -1, own.at[last], BH.at[j].at[low]),
            (-1, 1, own.at[first], BL.at[j].at[high]), (-1, -1, own.at[first], BH.at[j].at[high]),
        )

    cond_messages = (
        (1, 0, CTOP, CLO),
        (0, 1, BC, BCL.at[mid]),
        (1, 1, BC.at[pl.ds(R - 8, 8)], BCL.at[low]),
    )
    exchange(STEPS, cond_messages, True)
    exchange(STEPS, cond_messages, False)
    for x in range(X):
        for ref, k in ((C1, 3.0), (C2, 2.0), (C3, 1.0)):
            ref[x, LO - 1:LO, :] = CLO[x:x + 1, :] * k

    for r in chunks:
        low_z = BCL[r:r + 8, :] + BCL[r - 1:r + 7, :]
        low_z = low_z + jnp.where(lane16 >= 2, roll(low_z, 2), 0.0)
        before = None
        for x in range(X):
            t = C3[x, r:r + 8, :] + C3[x, r - 1:r + 7, :]
            both = t if before is None else t + before
            before = t
            below = jnp.where(lane == 0, roll(low_z, -2 * x), roll(both, 1))
            total = (both + below) * 48.0 / 3.0
            free = 1.0 - fixed[x, r - LO:r - LO + 8, :].astype(f32)
            DIAG[x, r - LO:r - LO + 8, :] = total
            INV[x, r - LO:r - LO + 8, :] = free / total

    def pack_tail(j, l, r, b):
        BO[j, r:r + 8, :] = jnp.where(group == l, b, BO[j, r:r + 8, :])

    def edges(j, l, x, r, v):
        if r == LO:
            EBOT[j, l, x:x + 1, :] = v[0:1, :]
        if r == HI - 8:
            ETOP[j, l, x:x + 1, :] = v[7:8, :]

    @pl.loop(0, L)
    def _(l):
        acc = zero
        for r in chunks:
            b = zero
            q = r - LO
            for x in range(X):
                inv = INV[x, q:q + 8, :]
                rhs = heat[l, x, q:q + 8, :] * source[x, q:q + 8, :].astype(f32)
                v = rhs * inv
                U[0][l, x, r:r + 8, :] = v
                acc = acc + v * v * DIAG[x, q:q + 8, :]
                b = jnp.where(lane16 >= 2 * x, roll(v, 16 * l + 2 * x + 1), b)
                edges(0, l, x, r, v)
            pack_tail(0, l, r, b)
        ACC[0, l] = acc
    exchange(0, halo(0), True)

    def fill(j):
        @pl.loop(0, L)
        def _(l):
            for x in range(X):
                U[j][l, x, LO - 1:LO, :] = ELO[j, l, x:x + 1, :]
                U[j][l, x, HI:HI + 1, :] = EHI[j, l, x:x + 1, :]

        def up_x(v):
            return jnp.where(lane16 < 14, roll(v, -2), 0.0)

        def down_x(v):
            return jnp.where(lane16 >= 2, roll(v, 2), 0.0)

        for r in (0,) + chunks:
            a0, a1 = BL[j, r:r + 8, :], BL[j, r + 1:r + 9, :]
            b0, b1 = roll(BO[j, r:r + 8, :], -1), roll(BO[j, r + 1:r + 9, :], -1)
            c = BCL[r:r + 8, :]
            pushes = []
            s0, d0, s1, d1 = a0 + b0, b0 - a0, a1 + b1, b1 - a1
            fields = ((s0 + s1, 0), (s1 - s0, 1), (d0 + d1, 1), (d1 - d0, 2))
            outs = []
            for f, k in fields:
                g = up_x(f)
                td = (g - f) * (c * float(3 - k))
                ts = None if k == 0 else (f + g) * (c * float(4 - k))
                if ts is None:
                    outs.append(down_x(td) - td)
                else:
                    outs.append(ts - td + down_x(ts + td))
            ss, sd, ds, dd = outs
            ps, pd = ss + ds, sd + dd
            WC[0, r:r + 8, :] = ps + pd
            if r:
                push = ps - pd + WC[0, r - 1:r + 7, :]
                push = roll(push, 1)
            else:
                push = zero
            W[j, r:r + 8, :] = jnp.where(lax.rem(lane, 2) == 0, roll(BH[j, r:r + 8, :], -1), push)
        W[j, HI:RP, :] = roll(BH[j, HI:RP, :], -1)

    def next_row(v, following):
        return pltpu.roll(jnp.where(sub == 0, following, v), 7, 0)

    def step(j):
        scale = 2.0 if j else 1.0

        @pl.loop(0, L)
        def _(l):
            back = 128 - (16 * l + 1)
            def chunk(r, above, sums):
                here, ahead = pl.ds(r, 8), pl.ds(r + 8, 8)
                if sums is not None:
                    here, ahead = pl.ds(pl.multiple_of(r, 8), 8), pl.ds(pl.multiple_of(r + 8, 8), 8)
                    owned = pl.ds(pl.multiple_of(r - LO, 8), 8)
                    acc_a, acc_b = sums
                w0 = W[j, here, :]
                w1 = next_row(w0, W[j, ahead, :])
                ws, wd = w0 + w1, w1 - w0

                def node(x):
                    u0 = U[j][l, x, here, :]
                    u1 = next_row(u0, U[j][l, x, ahead, :])
                    amount = back - 2 * x
                    ys, yd = u0 + u1, u1 - u0
                    ns = jnp.where(lane == 127, roll(ws, amount), roll(ys, 127))
                    nd = jnp.where(lane == 127, roll(wd, amount), roll(yd, 127))
                    return (ys + ns, yd + nd, ns - ys, nd - yd)

                now, carry, b = node(0), None, zero
                pushed, news = [], []
                for x in range(X):
                    nxt = node(x + 1) if x + 1 < X else None
                    cs = (C1[x, here, :], C2[x, here, :], C3[x, here, :])
                    outs, new_carry = [], []
                    for i, k in enumerate((0, 1, 1, 2)):
                        f = now[i]
                        if nxt is None:
                            d, s = -f, f
                        else:
                            d, s = nxt[i] - f, nxt[i] + f
                        td = d * cs[k]
                        if k == 0:
                            o, n = -td, td
                        else:
                            ts = s * cs[k - 1]
                            o, n = ts - td, ts + td
                        if carry is not None:
                            o = o + carry[i]
                        outs.append(o)
                        new_carry.append(n)
                    carry = new_carry
                    now = nxt
                    ss, sd, ds, dd = outs
                    ps, pd = ss + sd, ds + dd
                    pushed += [ps, pd]
                    if sums is None:
                        continue
                    es = ss - sd + pltpu.roll(jnp.where(sub == 7, above[2 * x], ps), 1, 0)
                    ed = ds - dd + pltpu.roll(jnp.where(sub == 7, above[2 * x + 1], pd), 1, 0)
                    push = jnp.where(lane == 0, roll(w0, back - 2 * x), roll(es + ed, 1))
                    image = es - ed + push
                    v = U[j][l, x, here, :]
                    new = image * (INV[x, owned, :] * (scale / HALF)) - scale * v
                    if j:
                        new = new - U[j - 1][l, x, here, :]
                    weighted = new * DIAG[x, owned, :]
                    acc_a = acc_a + v * weighted
                    if j + 1 < STEPS:
                        acc_b = acc_b + new * weighted
                        b = jnp.where(lane16 >= 2 * x, roll(new, 16 * l + 2 * x + 1), b)
                        news.append(new)
                if news:
                    for x, new in enumerate(news):
                        U[j + 1][l, x, here, :] = new
                    BO[j + 1, here, :] = jnp.where(group == l, b, BO[j + 1, here, :])
                if sums is None:
                    return tuple(pushed)
                return tuple(pushed), (acc_a, acc_b)

            _, (acc_a, acc_b) = lax.fori_loop(
                1, HI // 8, lambda c, carry: chunk(c * 8, *carry), (chunk(0, None, None), (zero, zero)), unroll=2)
            ACC[2 * j + 1, l] = acc_a
            if j + 1 < STEPS:
                ACC[2 * j + 2, l] = acc_b
                for x in range(X):
                    EBOT[j + 1, l, x:x + 1, :] = U[j + 1][l, x, LO:LO + 1, :]
                    ETOP[j + 1, l, x:x + 1, :] = U[j + 1][l, x, HI - 1:HI, :]

    for j in range(STEPS):
        exchange(j, halo(j), False)
        fill(j)
        step(j)
        if j + 1 < STEPS:
            exchange(j + 1, halo(j + 1), True)

    rows = zero
    for k in range(2 * STEPS):
        for l in range(L):
            t = jnp.sum(jnp.sum(ACC[k, l], axis=0, keepdims=True), axis=1, keepdims=True)
            rows = jnp.where((sub == k) & (lane == l), t, rows)

    def spread(buffer, n, axis_z, base):
        def copy(d):
            target = (my_y, lax.rem(my_z + d, nz)) if axis_z else (lax.rem(my_y + d, ny), my_z)
            return pltpu.make_async_remote_copy(
                src_ref=buffer.at[0], dst_ref=buffer.at[d], send_sem=rsend.at[base + d],
                recv_sem=rrecv.at[base + d], device_id=target, device_id_type=MESH)
        for d in range(1, n):
            copy(d).start()
        for d in range(1, n):
            copy(d).wait()
        total = buffer[0]
        for d in range(1, n):
            total = total + buffer[d]
        return total

    AZ[0] = rows
    AY[0] = spread(AZ, nz, True, 0)
    RED[...] = spread(AY, ny, False, nz)
    a = [RED[k:k + 1, :] for k in range(2 * STEPS)]
    m = [a[0], a[1]]
    for k in range(2, 2 * STEPS):
        m.append(2.0 * a[k] - m[k % 2])

    def gram(i, j):
        return 0.5 * (m[i + j] + m[abs(i - j)])

    def times_m(c):
        out = [None] * (len(c) + 1)
        def put(i, v):
            out[i] = v if out[i] is None else out[i] + v
        for i, v in enumerate(c):
            put(i, HALF * v)
            put(i + 1, (HALF if i == 0 else 0.5 * HALF) * v)
            if i:
                put(i - 1, 0.5 * HALF * v)
        return out

    def form(c, e):
        total = 0.0
        for i, v in enumerate(c):
            for k, w in enumerate(e):
                total = total + v * w * gram(i, k)
        return total

    one = jnp.ones((1, Z), f32)
    zc, dc, tc = [one], [one], []
    rz = form(zc, zc)
    for it in range(STEPS):
        image = times_m(dc)
        alpha = rz / form(dc, image)
        tc = [alpha * v + (tc[i] if i < len(tc) else 0.0) for i, v in enumerate(dc)]
        if it + 1 == STEPS:
            break
        zc = [(zc[i] if i < len(zc) else 0.0) - alpha * v for i, v in enumerate(image)]
        new = form(zc, zc)
        beta = new / rz
        dc = [v + (beta * dc[i] if i < len(dc) else 0.0) for i, v in enumerate(zc)]
        rz = new

    packed = [zero] * STEPS
    for i in range(STEPS):
        for l in range(L):
            t = jnp.sum(jnp.where(lane[0:1] == l, tc[i], 0.0), axis=1, keepdims=True)
            t = jnp.broadcast_to(t, (8, Z))
            COEF[i, l] = t
            packed[i] = jnp.where(group == l, t, packed[i])
    for r in chunks + (HI,):
        WC[0, r:r + 8, :] = sum(packed[i] * W[i, r:r + 8, :] for i in range(1, STEPS)) + packed[0] * W[0, r:r + 8, :]

    S[...] = jnp.zeros(S.shape, f32)

    @pl.loop(0, L)
    def _(l):
        cs = [COEF[i, l] for i in range(STEPS)]
        back = 128 - (16 * l + 1)
        for x in range(X):
            for r in chunks + (HI,):
                t = cs[0] * U[0][l, x, r:r + 8, :]
                for i in range(1, STEPS):
                    t = t + cs[i] * U[i][l, x, r:r + 8, :]
                PS[0, x, r:r + 8, :] = t
                if r < HI:
                    temp[l, x, r - LO:r - LO + 8, :] = t
        for r in chunks:
            w0, w1 = WC[0, r:r + 8, :], WC[0, r + 1:r + 9, :]
            ws, wd = w0 + w1, w1 - w0

            def node(x):
                u0, u1 = PS[0, x, r:r + 8, :], PS[0, x, r + 1:r + 9, :]
                amount = back - 2 * x
                ys, yd = u0 + u1, u1 - u0
                ns = jnp.where(lane == 127, roll(ws, amount), roll(ys, 127))
                nd = jnp.where(lane == 127, roll(wd, amount), roll(yd, 127))
                return (ys + ns, yd + nd, ns - ys, nd - yd)

            now = node(0)
            for x in range(X):
                nxt = node(x + 1) if x + 1 < X else (zero,) * 4
                groups = [None, None, None]
                for i, k in enumerate((0, 1, 1, 2)):
                    d = nxt[i] - now[i]
                    groups[k] = d * d if groups[k] is None else groups[k] + d * d
                    if k:
                        s = nxt[i] + now[i]
                        groups[k - 1] = groups[k - 1] + s * s
                now = nxt
                S[x, r:r + 8, :] += 3.0 * groups[0] + 2.0 * groups[1] + groups[2]

    def mass(index, total):
        out = jnp.zeros(index.shape, f32)
        for s in range(-3, 4):
            ok = (index + s >= 0) & (index + s < total)
            out = out + jnp.where(ok, 4.0 - abs(s), 0.0)
        return out

    mz = mass(my_z * Z + lane, nz * Z)
    for r in chunks:
        my = mass(my_y * R + (r - LO) + sub, ny * R)
        inv_yz = (-3.0 * (1.0 - FLOOR) / (48.0 * L)) / (my * mz)
        vs = []
        for x in range(X):
            density = (seed[x, r - LO:r - LO + 8, :].astype(f32) + 1.0) / 16.0
            mx = float(sum(4 - abs(s) for s in range(-3, 4) if 0 <= x + s < X))
            vs.append(S[x, r:r + 8, :] * (density * density) * inv_yz * (1.0 / mx))
        b = zero
        for x in range(X):
            v = 4.0 * vs[x]
            for s in (1, 2, 3):
                for o in (x - s, x + s):
                    if 0 <= o < X:
                        v = v + (4.0 - s) * vs[o]
            S[x, r:r + 8, :] = v
            b = jnp.where(lane >= 16 * x, roll(v, 16 * x + 8), b)
        PZ[r - LO:r - LO + 8, :] = b

    top, bottom = pl.ds(R - 8, 8), pl.ds(0, 8)
    final = (
        (1, 0, S.at[:, last], SLO), (-1, 0, S.at[:, first], SHI),
        (0, 1, PZ, PZL.at[mid]), (0, -1, PZ, PZH.at[mid]),
        (1, 1, PZ.at[top], PZL.at[low]), (1, -1, PZ.at[top], PZH.at[low]),
        (-1, 1, PZ.at[bottom], PZL.at[high]), (-1, -1, PZ.at[bottom], PZH.at[high]),
    )
    exchange(STEPS + 1, final, True)
    exchange(STEPS + 1, final, False)
    for x in range(X):
        S[x, 0:LO, :] = SLO[x]
        S[x, HI:RP, :] = SHI[x]
    for r in (0,) + chunks + (HI,):
        PM[r:r + 8, :] = jnp.where(lane16 < 8, PZL[r:r + 8, :], PZH[r:r + 8, :])

    def along_y(get):
        v = 4.0 * get(0)
        for s in (1, 2, 3):
            v = v + (4.0 - s) * (get(s) + get(-s))
        return v

    for r in chunks:
        pm = along_y(lambda s: PM[r + s:r + s + 8, :])
        for x in range(X):
            v = along_y(lambda s: S[x, r + s:r + s + 8, :])
            w = roll(pm, -(16 * x + 8))
            out = 4.0 * v
            for s in (1, 2, 3):
                up = jnp.where(lane >= 128 - s, roll(w, -s), roll(v, -s))
                down = jnp.where(lane < s, roll(w, s), roll(v, s))
                out = out + (4.0 - s) * (up + down)
            sens[x, r - LO:r - LO + 8, :] = out


def on_device(ny, nz, seed, heat, source, fixed):
    f32 = jnp.float32
    v = pltpu.VMEM
    scratch = [
        *(v((L, X, RP, Z), f32) for _ in range(STEPS)),
        v((STEPS, RP, Z), f32), v((STEPS, RP, Z), f32), v((STEPS, RP, Z), f32),
        v((STEPS, L, X, Z), f32), v((STEPS, L, X, Z), f32),
        v((STEPS, L, X, Z), f32), v((STEPS, L, X, Z), f32),
        v((STEPS, RP, Z), f32), v((1, RP, Z), f32),
        v((X, RP, Z), f32), v((X, RP, Z), f32), v((X, RP, Z), f32),
        v((X, R, Z), f32), v((X, R, Z), f32),
        v((1, X, RP, Z), f32),
        v((2 * STEPS, L, 8, Z), f32), v((8, Z), f32), v((STEPS, L, 8, Z), f32),
        v((R, Z), f32), v((RP, Z), f32), v((X, Z), f32), v((X, Z), f32),
        v((X, RP, Z), f32), v((X, 8, Z), f32), v((X, 8, Z), f32),
        v((R, Z), f32), v((RP, Z), f32), v((RP, Z), f32), v((RP, Z), f32),
        v((nz, 8, Z), f32), v((ny, 8, Z), f32),
        pltpu.SemaphoreType.DMA((STEPS + 2, 10)), pltpu.SemaphoreType.DMA((STEPS + 2, 10)),
        pltpu.SemaphoreType.DMA((ny + nz,)), pltpu.SemaphoreType.DMA((ny + nz,)),
    ]
    return pl.pallas_call(
        functools.partial(kernel, ny, nz),
        out_shape=(jax.ShapeDtypeStruct((L, X, R, Z), f32), jax.ShapeDtypeStruct((X, R, Z), f32)),
        in_specs=[pl.BlockSpec(memory_space=pltpu.VMEM)] * 4,
        out_specs=(pl.BlockSpec(memory_space=pltpu.VMEM),) * 2,
        scratch_shapes=scratch,
        compiler_params=pltpu.CompilerParams(
            collective_id=0, has_side_effects=True, vmem_limit_bytes=40 * 2**20
        ),
    )(seed, heat, source, fixed)


def solution(mesh):
    in_specs = (
        P(None, "gy", "gz"),
        P(None, None, "gy", "gz"),
        P(None, "gy", "gz"),
        P(None, "gy", "gz"),
    )
    out_specs = (P(None, None, "gy", "gz"), P(None, "gy", "gz"))
    body = functools.partial(on_device, mesh.shape["gy"], mesh.shape["gz"])
    return jax.shard_map(body, mesh=mesh, in_specs=in_specs, out_specs=out_specs, check_vma=False)
```
